128 devices in a mesh: ctx: 16 (over x, z_lo, core), head: 8 (over y, z_hi).
Axes of the slice: x: 4, y: 4, z: 4 (z_hi: 2, z_lo: 2; z = z_hi * 2 + z_lo), core: 2. Of those that a mesh axis runs over, the one named last changes fastest.
Arguments:
- queries: bfloat16 [4096, 64, 128], P('ctx', 'head'), may hold values from -120 to 120
- keys: bfloat16 [4096, 8, 128], P('ctx', 'head'), may hold values from -5 to 5
- values: bfloat16 [4096, 8, 128], P('ctx', 'head'), may hold values from -6 to 6
- forward_out: bfloat16 [4096, 64, 128], P('ctx', 'head'), may hold values from -6 to 6
- grad_out: bfloat16 [4096, 5120], P('ctx', 'head'), may hold values from -6 to 6
- out_weight: bfloat16 [8192, 5120], P('head'), may hold values from -0.078125 to 0.078125
- block_docs: int32 [32], replicated, may hold values from 0 to 7, never falling along the last dimension, each value on 1 to 24 neighbouring positions
- doc_group: int32 [8], replicated, may hold values from 0 to 3, as said below
- prefix_keys: bfloat16 [1024, 8, 128], P('ctx', 'head'), may hold values from -6 to 6
- prefix_values: bfloat16 [1024, 8, 128], P('ctx', 'head'), may hold values from -6 to 6
Outputs:
- query_grad: bfloat16 [4096, 64, 128], P('ctx', 'head')
- key_grad: bfloat16 [4096, 8, 128], P('ctx', 'head')
- value_grad: bfloat16 [4096, 8, 128], P('ctx', 'head')
- prompt_key_grad: bfloat16 [1024, 8, 128], P('ctx', 'head')
- prompt_value_grad: bfloat16 [1024, 8, 128], P('ctx', 'head')
The draws below stay inside these ranges and needn't reach their ends.
Inputs may be any that keep to these rules, and one draw needn't show every extreme that they name: `block_docs`: ids never fall from block to block; each document covers 1 to 24 consecutive blocks and one covers exactly 24. `doc_group`: each group is answered by exactly 2 documents.
All inputs are finite; a program needn't handle non-finite values.
Results may differ from the reference program's by a relative error of at most 0.01.
Values may be sent and summed in bfloat16 or wider, within the bound.
No kernel may reach another device: no remote copies, remote signals or barrier semaphores. Data moves between devices by JAX's collectives and lax.ppermute only.
A program may use at most 128 MiB of HBM per device.

```python
import math
import jax
import jax.numpy as jnp
import numpy as np
from jax import lax

D = 5120
KVH = 8
QPK = 8
HD = 128
BLK = 128
HQ = 64
TOKENS = 4096
NBLK = 32
MOSTB = 24
NDOCS = 8
NGROUPS = 4
PTOK = 1024
PLEN = 256


def keys_base(key):
    return jnp.clip(jax.random.normal(jax.random.fold_in(key, 11), (TOKENS, KVH, HD), jnp.float32), -5.0, 5.0)


def draw_keys(key, part):
    base = keys_base(key)
    return base.astype(jnp.bfloat16)


def draw_queries(key, part):
    key = jax.random.fold_in(key, 5)
    fresh = jnp.clip(jax.random.normal(key, (TOKENS, HQ, HD), jnp.float32), -5.0, 5.0)
    return fresh.astype(jnp.bfloat16)


def draw_doc_group(key, part):
    key = jax.random.fold_in(key, 7)
    order = jax.random.permutation(key, NDOCS)
    return (order % NGROUPS).astype(jnp.int32)


def level_of(own_key, dims, cuts, low, high):
    factor_of, own = 1.0, jax.random.fold_in(own_key, 6)
    for axis_at, shards_of in cuts:
        draws = jnp.exp(jax.random.uniform(jax.random.fold_in(own, axis_at), (shards_of,), jnp.float32, low / len(cuts), high / len(cuts)))
        factor_of = factor_of * jnp.repeat(draws, dims[axis_at] // shards_of).reshape([-1 if axis == axis_at else 1 for axis in range(len(dims))])
    return factor_of


def length_profile(count, total, reach, skew):
    weights = [(1 << 20) // math.isqrt(grade ** skew) + 1 for grade in range(2, count + 1)]
    surplus, holding = total - reach - (count - 1), [1] * (count - 1)
    while surplus > 0:
        free = [i for i in range(count - 1) if holding[i] < reach]
        pool, remaining = sum([weights[i] for i in free]), surplus
        for i in free:
            extra = min(reach - holding[i], max(1, remaining * weights[i] // pool), surplus)
            holding[i] = holding[i] + extra
            surplus = surplus - extra
    return np.array([reach] + holding)


def ragged_sizes(rng, amount, total, most, skew):
    if amount == 2:
        one = jax.random.randint(rng, (), max(1, total - most), min(most, total - 1) + 1)
        return jnp.stack([one, total - one])
    sizes = jnp.asarray(length_profile(amount, total, most, skew), jnp.int32)
    pairs = (amount - 1) // 2
    donor, receiver = sizes[1:1 + 2 * pairs:2], sizes[2:2 + 2 * pairs:2]
    room = jnp.minimum(donor - 1, most - receiver)
    passed = jax.random.randint(jax.random.fold_in(rng, 1), (pairs,), 0, 1 << 20) % (room + 1)
    sizes = sizes.at[1:1 + 2 * pairs:2].set(donor - passed).at[2:2 + 2 * pairs:2].set(receiver + passed)
    return sizes[jax.random.permutation(jax.random.fold_in(rng, 2), amount)]


def bell_draw(stream_key, shape, deviation, bound, cuts=(), kind=jnp.bfloat16):
    values = jax.random.normal(stream_key, shape, jnp.float32) * deviation
    if len(cuts) > 0:
        values = level_of(stream_key, shape, cuts, -0.22, 0.18) * values
    return jnp.clip(values, min=-bound, max=bound).astype(kind)


def setup_inputs(seed: int = 0) -> dict:
    seeds = jax.random.split(jax.random.key(seed), 11)
    queries = draw_queries(jax.random.fold_in(seeds[10], 71), 0)
    keys = draw_keys(jax.random.fold_in(seeds[10], 71), 0)
    values = bell_draw(seeds[2], (TOKENS, KVH, HD), 1.0, 6.0, ((0, 16), (1, 8)))
    forward_out = bell_draw(seeds[3], (TOKENS, HQ, HD), 1.0, 6.0, ((0, 16), (1, 8)))
    grad_out = bell_draw(seeds[4], (TOKENS, D), 1.0, 6.0, ((0, 16), (1, 8)))
    out_weight = bell_draw(seeds[5], (HQ * HD, D), D ** -0.5, 0.078125, ((0, 8),))
    block_docs = jnp.searchsorted(jnp.cumsum(ragged_sizes(seeds[6], NDOCS, NBLK, MOSTB, 0)), jnp.arange(NBLK), side="right").astype(jnp.int32)
    doc_group = draw_doc_group(jax.random.fold_in(seeds[10], 71), 0)
    prefix_keys = bell_draw(seeds[8], (PTOK, KVH, HD), 1.0, 6.0, ((0, 16), (1, 8)))
    prefix_values = bell_draw(seeds[9], (PTOK, KVH, HD), 1.0, 6.0, ((0, 16), (1, 8)))
    return dict(queries=queries, keys=keys, values=values, forward_out=forward_out, grad_out=grad_out, out_weight=out_weight, block_docs=block_docs, doc_group=doc_group, prefix_keys=prefix_keys, prefix_values=prefix_values)


NEGATIVE = -1e30


def reference(queries, keys, values, forward_out, grad_out, out_weight, block_docs, doc_group, prefix_keys, prefix_values):
    factor = HD ** -0.5
    grad_heads = jnp.dot(grad_out, out_weight.T, preferred_element_type=jnp.float32).astype(jnp.bfloat16)
    grad_heads = grad_heads.reshape(TOKENS, HQ, HD)
    delta = jnp.sum(grad_heads.astype(jnp.float32) * forward_out.astype(jnp.float32), axis=2)
    token_docs = jnp.repeat(block_docs, BLK)
    positions = jnp.arange(TOKENS, dtype=jnp.int32)
    visible = (token_docs[:, None] == token_docs[None, :]) & (positions[None, :] <= positions[:, None])
    query_groups = jnp.take(doc_group, token_docs)
    prompt_visible = query_groups[:, None] == (jnp.arange(PTOK, dtype=jnp.int32) // PLEN)[None, :]
    visible_all = jnp.concatenate([visible, prompt_visible], axis=1)
    keys_all = jnp.concatenate([keys, prefix_keys], axis=0)
    values_all = jnp.concatenate([values, prefix_values], axis=0)

    def one_head(head):
        group = head // QPK
        query = lax.dynamic_index_in_dim(queries, head, 1, keepdims=False)
        grad_row = lax.dynamic_index_in_dim(grad_heads, head, 1, keepdims=False)
        delta_row = lax.dynamic_index_in_dim(delta, head, 1, keepdims=False)
        key_mat = lax.dynamic_index_in_dim(keys_all, group, 1, keepdims=False)
        value_mat = lax.dynamic_index_in_dim(values_all, group, 1, keepdims=False)
        score = jnp.dot(query, key_mat.T, preferred_element_type=jnp.float32) * factor
        highest = jnp.max(jnp.where(visible_all, score, NEGATIVE), axis=1)
        totals = jnp.sum(jnp.where(visible_all, jnp.exp(score - highest[:, None]), 0.0), axis=1)
        lse = highest + jnp.log(totals)
        prob = jnp.where(visible_all, jnp.exp(score - lse[:, None]), 0.0)
        dprob = jnp.dot(grad_row, value_mat.T, preferred_element_type=jnp.float32)
        dscore = (prob * (dprob - delta_row[:, None])).astype(jnp.bfloat16)
        prob_low = prob.astype(jnp.bfloat16)
        grad_query = factor * jnp.dot(dscore, key_mat, preferred_element_type=jnp.float32)
        grad_key = jnp.dot(dscore.T, query, preferred_element_type=jnp.float32)
        grad_value = jnp.dot(prob_low.T, grad_row, preferred_element_type=jnp.float32)
        return grad_query, grad_key, grad_value

    head_ids = jnp.arange(HQ, dtype=jnp.int32)
    grad_query, grad_key, grad_value = lax.map(one_head, head_ids)
    grad_key = jnp.sum(grad_key.reshape(KVH, QPK, TOKENS + PTOK, HD), axis=1)
    grad_value = jnp.sum(grad_value.reshape(KVH, QPK, TOKENS + PTOK, HD), axis=1)
    query_grad = jnp.transpose(grad_query, (1, 0, 2)).astype(jnp.bfloat16)
    key_all = (factor * jnp.transpose(grad_key, (1, 0, 2))).astype(jnp.bfloat16)
    value_all = jnp.transpose(grad_value, (1, 0, 2)).astype(jnp.bfloat16)
    return query_grad, key_all[:TOKENS], value_all[:TOKENS], key_all[TOKENS:], value_all[TOKENS:]
```

```python
import functools

import jax
import jax.numpy as jnp
from jax import lax
from jax.experimental import pallas as pl
from jax.experimental.pallas import tpu as pltpu
from jax.sharding import PartitionSpec as P

BLK = 128
NBLK = 32
NDOCS = 8
HD = 128
CHUNK = 256
PCHUNK = 64
ROWS = 2048
HALF = 1024
TOKENS = 4096
PTOK = 1024
PLEN = 256
DLOC = 640
PIECE = CHUNK + PCHUNK

FACTOR = HD ** -0.5
LOG2E = 1.4426950408889634
SCALE2 = FACTOR * LOG2E
NEGATIVE = -1e30

PARTS = ((0, 256, (6, 1, 2)), (256, 256, (1, 2, 6)), (512, 128, (2, 6, 1)))

BF = jnp.bfloat16
F32 = jnp.float32


def masks_of(order):
    masks = [0]
    for step in order:
        masks = masks + [mask ^ step for mask in masks]
    return masks


def dot(a, b, ca, cb):
    return lax.dot_general(a, b, (((ca,), (cb,)), ((), ())), preferred_element_type=F32)


def swap_ctx(value, move):
    return lax.ppermute(value, "ctx", [(i, move(i)) for i in range(16)])


def swap_head(value, mask):
    return lax.ppermute(value, "head", [(i, i ^ mask) for i in range(8)])


def x_shift(steps):
    return lambda i: ((i // 4 + steps) % 4) * 4 + i % 4


def core_swap(i):
    return i ^ 1


def z_swap(i):
    return i ^ 2


def gather_ctx(own):
    pair = jnp.stack([own, swap_ctx(own, z_swap)])
    from_next = swap_ctx(pair, x_shift(-1))
    from_prev = swap_ctx(pair, x_shift(1))
    from_far = swap_ctx(pair, x_shift(2))
    same = jnp.stack([pair, from_next, from_far, from_prev])
    return same, swap_ctx(same, core_swap)


def ctx_of(me, s, i, other):
    x = (me // 4 + s) % 4
    z = (me // 2) % 2
    core = me % 2
    z = 1 - z if i else z
    core = 1 - core if other else core
    return x * 4 + z * 2 + core


def assemble(me, same, other, packed, prompt):
    for which, ref in ((0, same), (1, other)):
        for s in range(4):
            for i in range(2):
                at = ctx_of(me, s, i, which)
                packed[pl.ds(pl.multiple_of(at * CHUNK, CHUNK), CHUNK), :] = ref[s, i, :CHUNK, :]
                prompt[pl.ds(pl.multiple_of(at * PCHUNK, PCHUNK), PCHUNK), :] = ref[s, i, CHUNK:, :]


def block_facts(docs, groups, block):
    doc = docs[block]
    start = jnp.int32(0)
    for j in range(NBLK):
        start = start + (docs[j] < doc).astype(jnp.int32)
    return start, groups[doc]


def causal():
    keys = lax.broadcasted_iota(jnp.int32, (BLK, HALF), 0)
    toks = lax.broadcasted_iota(jnp.int32, (BLK, HALF), 1) >> 3
    return keys <= toks


def rows_at(first, count):
    return pl.ds(pl.multiple_of(first, BLK), count)


def lse_kernel(me_ref, docs, groups, q_ref, same, other, lse_ref, kall, pall):
    me = me_ref[0]
    assemble(me, same, other, kall, pall)
    for half in range(2):
        block = 2 * me + half
        start, group = block_facts(docs, groups, block)
        q = q_ref[half * HALF : (half + 1) * HALF, :]

        def fold(keys, state, masked):
            score = dot(keys, q, 1, 1) * SCALE2
            if masked:
                score = jnp.where(causal(), score, NEGATIVE)
            score = score.reshape(-1, 8, HALF)
            high = jnp.max(score, axis=0)
            if state is None:
                return high, jnp.sum(jnp.exp2(score - high[None]), axis=0)
            top, total = state
            new = jnp.maximum(top, high)
            return new, total * jnp.exp2(top - new) + jnp.sum(jnp.exp2(score - new[None]), axis=0)

        state = fold(pall[rows_at(group * PLEN, PLEN), :], None, False)
        state = fold(kall[rows_at(block * BLK, BLK), :], state, True)
        count = block - start
        state = lax.fori_loop(
            0,
            count // 2,
            lambda i, st: fold(kall[rows_at((start + 2 * i) * BLK, 2 * BLK), :], st, False),
            state,
        )
        state = lax.fori_loop(
            0,
            count % 2,
            lambda i, st: fold(kall[rows_at((block - 1) * BLK, BLK), :], st, False),
            state,
        )
        top, total = state
        best = jnp.max(top, axis=0, keepdims=True)
        whole = jnp.sum(total * jnp.exp2(top - best), axis=0, keepdims=True)
        lse_ref[:, half * HALF : (half + 1) * HALF] = best + jnp.log2(whole)


def weight_copies(head, weight, held, sems, lo):
    copies = []
    for p, (offset, width, order) in enumerate(PARTS):
        for k, mask in enumerate(masks_of(order)[lo : lo + 4]):
            source = pl.multiple_of((head ^ mask) * DLOC + offset, 128)
            at = 4 * offset + k * width
            copies.append(
                pltpu.make_async_copy(
                    weight.at[:, pl.ds(source, width)],
                    held.at[:, at : at + width],
                    sems.at[4 * p + k],
                )
            )
    return copies


def weight_dots(pieces, held, copies, total):
    for p, (offset, width, order) in enumerate(PARTS):
        for k in range(4):
            at = 4 * offset + k * width
            copies[4 * p + k].wait()
            term = dot(pieces[p][k], held[:, at : at + width], 1, 1)
            total = term if total is None else total + term
    return total


def early_kernel(head_ref, a0, a1, a2, weight, out, held, sems):
    copies = weight_copies(head_ref[0], weight, held, sems, 0)
    for copy in copies:
        copy.start()
    out[...] = weight_dots((a0, a1, a2), held, copies, None)


def main_kernel(
    me_ref, head_ref, docs, groups,
    early, a0, a1, a2, weight, q_ref, o_ref, lse_ref,
    ksame, kother, vsame, vother,
    dq_ref, keep_ref, send_ref,
    held, sems, g3, g_ref, delta_ref, kall, pkall, vall, pvall, dk, dv, dpk, dpv, dq_acc,
):
    me = me_ref[0]
    copies = weight_copies(head_ref[0], weight, held, sems, 4)
    for copy in copies:
        copy.start()
    assemble(me, ksame, kother, kall, pkall)
    assemble(me, vsame, vother, vall, pvall)
    for ref in (dk, dv, dpk, dpv, dq_acc):
        ref[...] = jnp.zeros_like(ref)
    total = weight_dots((a0, a1, a2), held, copies, early[...])
    for h in range(8):
        g3[:, h, :] = total[:, h * HD : (h + 1) * HD]
    for half in range(2):
        at = slice(half * HALF, (half + 1) * HALF)
        low = g3[half * BLK : (half + 1) * BLK].reshape(HALF, HD).astype(BF)
        g_ref[at, :] = low
        product = low.astype(F32) * o_ref[at, :].astype(F32)
        delta_ref[:, at] = jnp.sum(product.T, axis=0, keepdims=True)

    for half in range(2):
        block = 2 * me + half
        start, group = block_facts(docs, groups, block)
        at = slice(half * HALF, (half + 1) * HALF)
        lse = lse_ref[:, at]
        delta = delta_ref[:, at]

        def tile(keys_ref, vals_ref, dk_ref, dv_ref, rows, masked):
            q = q_ref[at, :]
            g = g_ref[at, :]
            keys = keys_ref[rows, :]
            vals = vals_ref[rows, :]
            prob = jnp.exp2(dot(keys, q, 1, 1) * SCALE2 - lse)
            if masked:
                prob = jnp.where(causal(), prob, 0.0)
            dprob = dot(vals, g, 1, 1)
            dscore = (prob * (dprob - delta)).astype(BF)
            dv_ref[rows, :] += dot(prob.astype(BF), g, 1, 0)
            dk_ref[rows, :] += dot(dscore, q, 1, 0)
            dq_acc[at, :] += dot(dscore, keys, 0, 0)

        tile(pkall, pvall, dpk, dpv, rows_at(group * PLEN, PLEN), False)
        tile(kall, vall, dk, dv, rows_at(block * BLK, BLK), True)
        count = block - start

        def pair(i, carry):
            tile(kall, vall, dk, dv, rows_at((start + 2 * i) * BLK, 2 * BLK), False)
            return carry

        def single(i, carry):
            tile(kall, vall, dk, dv, rows_at((block - 1) * BLK, BLK), False)
            return carry

        lax.fori_loop(0, count // 2, pair, 0)
        lax.fori_loop(0, count % 2, single, 0)
        dq_ref[at, :] = (dq_acc[at, :] * FACTOR).astype(BF)

    for which, ref in ((0, keep_ref), (1, send_ref)):
        for s in range(4):
            for i in range(2):
                to = ctx_of(me, s, i, which)
                big = pl.ds(pl.multiple_of(to * CHUNK, CHUNK), CHUNK)
                small = pl.ds(pl.multiple_of(to * PCHUNK, PCHUNK), PCHUNK)
                ref[s, i, 0:CHUNK, :] = dk[big, :].astype(BF)
                ref[s, i, CHUNK:PIECE, :] = dpk[small, :].astype(BF)
                ref[s, i, PIECE : PIECE + CHUNK, :] = dv[big, :].astype(BF)
                ref[s, i, PIECE + CHUNK :, :] = dpv[small, :].astype(BF)


def vmem():
    return pl.BlockSpec(memory_space=pltpu.VMEM)


def smem():
    return pl.BlockSpec(memory_space=pltpu.SMEM)


def anywhere():
    return pl.BlockSpec(memory_space=pl.ANY)


def per_device(
    queries, keys, values, forward_out, grad_out, out_weight,
    block_docs, doc_group, prefix_keys, prefix_values,
):
    me = lax.axis_index("ctx").astype(jnp.int32).reshape(1)
    head = lax.axis_index("head").astype(jnp.int32).reshape(1)
    q = queries.reshape(ROWS, HD)
    o = forward_out.reshape(ROWS, HD)

    held = [grad_out[:, offset : offset + width][None] for offset, width, _ in PARTS]
    first = [swap_head(held[p], PARTS[p][2][0]) for p in range(3)]
    held = [jnp.concatenate([held[p], first[p]]) for p in range(3)]
    k_own = jnp.concatenate([keys[:, 0], prefix_keys[:, 0]])
    v_own = jnp.concatenate([values[:, 0], prefix_values[:, 0]])
    k_same, k_other = gather_ctx(k_own)
    second = [swap_head(held[p], PARTS[p][2][1]) for p in range(3)]
    held = [jnp.concatenate([held[p], second[p]]) for p in range(3)]
    v_same, v_other = gather_ctx(v_own)
    last = [swap_head(held[p], PARTS[p][2][2]) for p in range(3)]

    params = functools.partial(pltpu.CompilerParams, vmem_limit_bytes=56 * 1024 * 1024)

    lse = pl.pallas_call(
        lse_kernel,
        out_shape=jax.ShapeDtypeStruct((1, ROWS), F32),
        in_specs=[smem()] * 3 + [vmem()] * 3,
        out_specs=vmem(),
        scratch_shapes=[pltpu.VMEM((TOKENS, HD), BF), pltpu.VMEM((PTOK, HD), BF)],
        compiler_params=params(),
        cost_estimate=pl.CostEstimate(flops=3 * 10**9, bytes_accessed=3 * 10**6, transcendentals=10**7),
        name="lse",
    )(me, block_docs, doc_group, q, k_same, k_other)

    early = pl.pallas_call(
        early_kernel,
        out_shape=jax.ShapeDtypeStruct((CHUNK, HALF), F32),
        in_specs=[smem()] + [vmem()] * 3 + [anywhere()],
        out_specs=vmem(),
        scratch_shapes=[pltpu.VMEM((HALF, 4 * DLOC), BF), pltpu.SemaphoreType.DMA((12,))],
        compiler_params=params(),
        cost_estimate=pl.CostEstimate(flops=14 * 10**8, bytes_accessed=8 * 10**6, transcendentals=0),
        name="early_grad",
    )(head, *held, out_weight)

    part = jax.ShapeDtypeStruct((4, 2, 2 * PIECE, HD), BF)
    dq, keep, send = pl.pallas_call(
        main_kernel,
        out_shape=(jax.ShapeDtypeStruct((ROWS, HD), BF), part, part),
        in_specs=[smem()] * 4 + [vmem()] * 4 + [anywhere()] + [vmem()] * 7,
        out_specs=(vmem(), vmem(), vmem()),
        scratch_shapes=[
            pltpu.VMEM((HALF, 4 * DLOC), BF),
            pltpu.SemaphoreType.DMA((12,)),
            pltpu.VMEM((CHUNK, 8, HD), F32),
            pltpu.VMEM((ROWS, HD), BF),
            pltpu.VMEM((1, ROWS), F32),
            pltpu.VMEM((TOKENS, HD), BF),
            pltpu.VMEM((PTOK, HD), BF),
            pltpu.VMEM((TOKENS, HD), BF),
            pltpu.VMEM((PTOK, HD), BF),
            pltpu.VMEM((TOKENS, HD), F32),
            pltpu.VMEM((TOKENS, HD), F32),
            pltpu.VMEM((PTOK, HD), F32),
            pltpu.VMEM((PTOK, HD), F32),
            pltpu.VMEM((ROWS, HD), F32),
        ],
        compiler_params=params(),
        cost_estimate=pl.CostEstimate(flops=10**10, bytes_accessed=10**7, transcendentals=10**7),
        name="attention_grads",
    )(me, head, block_docs, doc_group, early, *last, out_weight, q, o, lse, k_same, k_other, v_same, v_other)

    got = swap_ctx(send, core_swap)
    both = (keep.astype(F32) + got.astype(F32)).astype(BF)
    to_next = swap_ctx(both[1], x_shift(1))
    to_prev = swap_ctx(both[3], x_shift(-1))
    to_far = swap_ctx(both[2], x_shift(2))
    summed = both[0].astype(F32) + to_next.astype(F32) + to_prev.astype(F32) + to_far.astype(F32)
    final = summed[0] + swap_ctx(summed[1].astype(BF), z_swap).astype(F32)
    key_part = (FACTOR * final[:PIECE]).astype(BF)[:, None]
    value_part = final[PIECE:].astype(BF)[:, None]
    return (
        dq.reshape(CHUNK, 8, HD),
        key_part[:CHUNK],
        value_part[:CHUNK],
        key_part[CHUNK:],
        value_part[CHUNK:],
    )


def solution(mesh):
    tokens = P("ctx", "head", None)
    in_specs = (
        tokens, tokens, tokens, tokens, P("ctx", "head"), P("head", None), P(), P(), tokens, tokens,
    )
    return jax.shard_map(
        per_device, mesh=mesh, in_specs=in_specs, out_specs=(tokens,) * 5, check_vma=False
    )
```

```python
import jax
import jax.numpy as jnp
from jax import lax
from jax.experimental import pallas as pl
from jax.experimental.pallas import tpu as pltpu
from jax.sharding import PartitionSpec as P

BLK = 128
NBLK = 32
NDOCS = 8
HD = 128
CHUNK = 256
PCHUNK = 64
ROWS = 2048
HALF = 1024
TOKENS = 4096
PTOK = 1024
PLEN = 256
DLOC = 640
PIECE = CHUNK + PCHUNK

FACTOR = HD ** -0.5
LOG2E = 1.4426950408889634
SCALE2 = FACTOR * LOG2E
NEGATIVE = -1e30

BF = jnp.bfloat16
F32 = jnp.float32


def dot(a, b, ca, cb):
    return lax.dot_general(a, b, (((ca,), (cb,)), ((), ())), preferred_element_type=F32)


def swap_ctx(value, move):
    return lax.ppermute(value, "ctx", [(i, move(i)) for i in range(16)])


def head_of(head, dy, dz):
    return ((head // 2 + dy) % 4) * 2 + (head % 2 + dz) % 2


def from_head(value, dy, dz):
    return lax.ppermute(value, "head", [(head_of(i, dy, dz), i) for i in range(8)])


def x_shift(steps):
    return lambda i: ((i // 4 + steps) % 4) * 4 + i % 4


def core_swap(i):
    return i ^ 1


def z_swap(i):
    return i ^ 2


def ctx_of(me, s, i, other):
    x = (me // 4 + s) % 4
    z = (me // 2) % 2
    core = me % 2
    z = 1 - z if i else z
    core = 1 - core if other else core
    return x * 4 + z * 2 + core


def assemble(me, same, other, kall, pkall, vall, pvall):
    for which, ref in ((0, same), (1, other)):
        for s in range(4):
            for i in range(2):
                at = ctx_of(me, s, i, which)
                big = pl.ds(pl.multiple_of(at * CHUNK, CHUNK), CHUNK)
                small = pl.ds(pl.multiple_of(at * PCHUNK, PCHUNK), PCHUNK)
                kall[big, :] = ref[s, i, :CHUNK, :]
                pkall[small, :] = ref[s, i, CHUNK:PIECE, :]
                vall[big, :] = ref[s, i, PIECE : PIECE + CHUNK, :]
                pvall[small, :] = ref[s, i, PIECE + CHUNK :, :]


def block_facts(docs, groups, block):
    doc = docs[block]
    start = jnp.int32(0)
    for j in range(NBLK):
        start = start + (docs[j] < doc).astype(jnp.int32)
    return start, groups[doc]


def own_tokens(alike):
    keys = lax.broadcasted_iota(jnp.int32, (CHUNK, ROWS), 0)
    toks = lax.broadcasted_iota(jnp.int32, (CHUNK, ROWS), 1) >> 3
    first = jnp.where(alike, 0, toks >> 7 << 7)
    return (keys <= toks) & (keys >= first)


def rows_at(first, count):
    return pl.ds(pl.multiple_of(first, BLK), count)


PLACES = ((0, 0), (1, 0), (-1, 0), (0, 1), (1, 1), (-1, 1), (2, 0), (2, 1))


BOTH = slice(0, ROWS)
HALVES = (slice(0, HALF), slice(HALF, ROWS))


def walk(me, docs, groups, prompt, packed):
    start, group = block_facts(docs, groups, 2 * me)
    other_start, other_group = block_facts(docs, groups, 2 * me + 1)
    alike = docs[2 * me] == docs[2 * me + 1]
    prompt(HALVES[0], rows_at(group * PLEN, PLEN))
    prompt(HALVES[1], rows_at(other_group * PLEN, PLEN))
    packed(BOTH, pl.ds(pl.multiple_of(me * CHUNK, CHUNK), CHUNK), alike)
    count = 2 * me - start
    pairs, singles = count // 2, count % 2
    for columns, wanted in ((BOTH, alike), (HALVES[0], jnp.logical_not(alike))):

        def pair(i, carry):
            packed(columns, rows_at((start + 2 * i) * BLK, 2 * BLK), None)
            return carry

        def single(i, carry):
            packed(columns, rows_at((2 * me - 1) * BLK, BLK), None)
            return carry

        lax.fori_loop(0, jnp.where(wanted, pairs, 0), pair, 0)
        lax.fori_loop(0, jnp.where(wanted, singles, 0), single, 0)


def main_kernel(me_ref, head_ref, docs, groups, *refs):
    pieces = refs[:8]
    (weight, q_ref, o_ref, same, other, dq_ref, keep_ref, send_ref,
     held, grads, sems, g3, g_ref, delta_ref, lse_ref, tops, totals,
     kall, pkall, vall, pvall, dk, dv, dpk, dpv, dq_acc) = refs[8:]
    me = me_ref[0]
    copies = []
    for k, place in enumerate(PLACES):
        source = pl.multiple_of(head_of(head_ref[0], *place) * DLOC, 128)
        at = pl.ds(k * DLOC, DLOC)
        copies.append(
            pltpu.make_async_copy(weight.at[:, pl.ds(source, DLOC)], held.at[:, at], sems.at[k])
        )
        copies.append(pltpu.make_async_copy(pieces[k], grads.at[:, at], sems.at[8 + k]))
    for copy in copies:
        copy.start()
    assemble(me, same, other, kall, pkall, vall, pvall)
    for ref in (dk, dv, dpk, dpv, dq_acc):
        ref[...] = jnp.zeros_like(ref)

    def prompt_sums(columns, rows):
        score = dot(pkall[rows, :], q_ref[columns, :], 1, 1) * SCALE2
        score = score.reshape(PLEN // 8, 8, HALF)
        high = jnp.max(score, axis=0)
        tops[:, columns] = high
        totals[:, columns] = jnp.sum(jnp.exp2(score - high[None]), axis=0)

    def packed_sums(columns, rows, alike):
        score = dot(kall[rows, :], q_ref[columns, :], 1, 1) * SCALE2
        if alike is not None:
            score = jnp.where(own_tokens(alike), score, NEGATIVE)
        score = score.reshape(score.shape[0] // 8, 8, score.shape[1])
        top = tops[:, columns]
        new = jnp.maximum(top, jnp.max(score, axis=0))
        part = jnp.sum(jnp.exp2(score - new[None]), axis=0)
        totals[:, columns] = totals[:, columns] * jnp.exp2(top - new) + part
        tops[:, columns] = new

    walk(me, docs, groups, prompt_sums, packed_sums)
    top = tops[...]
    best = jnp.max(top, axis=0, keepdims=True)
    whole = jnp.sum(totals[...] * jnp.exp2(top - best), axis=0, keepdims=True)
    lse_ref[...] = best + jnp.log2(whole)

    for copy in copies:
        copy.wait()
    total = dot(grads[...], held[...], 1, 1)
    for h in range(8):
        g3[:, h, :] = total[:, h * HD : (h + 1) * HD]
    for half, at in enumerate(HALVES):
        low = g3[half * BLK : (half + 1) * BLK].reshape(HALF, HD).astype(BF)
        g_ref[at, :] = low
        product = low.astype(F32) * o_ref[at, :].astype(F32)
        delta_ref[:, at] = jnp.sum(product.T, axis=0, keepdims=True)

    def tile(keys_ref, vals_ref, dk_ref, dv_ref, columns, rows, alike):
        q = q_ref[columns, :]
        g = g_ref[columns, :]
        keys = keys_ref[rows, :]
        prob = jnp.exp2(dot(keys, q, 1, 1) * SCALE2 - lse_ref[:, columns])
        if alike is not None:
            prob = jnp.where(own_tokens(alike), prob, 0.0)
        dprob = dot(vals_ref[rows, :], g, 1, 1)
        dscore = (prob * (dprob - delta_ref[:, columns])).astype(BF)
        dv_ref[rows, :] += dot(prob.astype(BF), g, 1, 0)
        dk_ref[rows, :] += dot(dscore, q, 1, 0)
        dq_acc[:, columns] += dot(keys.T, dscore, 1, 0)

    def prompt_grads(columns, rows):
        tile(pkall, pvall, dpk, dpv, columns, rows, None)

    def packed_grads(columns, rows, alike):
        tile(kall, vall, dk, dv, columns, rows, alike)

    walk(me, docs, groups, prompt_grads, packed_grads)
    for at in HALVES:
        dq_ref[at, :] = (dq_acc[:, at].T * FACTOR).astype(BF)

    core = me % 2
    for which, ref in ((core, keep_ref), (1 - core, send_ref)):
        for j in range(8):
            to = 2 * j + which
            big = pl.ds(pl.multiple_of(to * CHUNK, CHUNK), CHUNK)
            small = pl.ds(pl.multiple_of(to * PCHUNK, PCHUNK), PCHUNK)
            ref[j, :CHUNK, :] = dk[big, :].astype(BF)
            ref[j, CHUNK:PIECE, :] = dpk[small, :].astype(BF)
            ref[j, PIECE : PIECE + CHUNK, :] = dv[big, :].astype(BF)
            ref[j, PIECE + CHUNK :, :] = dpv[small, :].astype(BF)


def sum_kernel(terms, k_ref, v_ref, pk_ref, pv_ref):
    total = terms[0].astype(F32)
    for j in range(1, 8):
        total = total + terms[j].astype(F32)
    k_ref[...] = (total[:CHUNK] * FACTOR).astype(BF)
    pk_ref[...] = (total[CHUNK:PIECE] * FACTOR).astype(BF)
    v_ref[...] = total[PIECE : PIECE + CHUNK].astype(BF)
    pv_ref[...] = total[PIECE + CHUNK :].astype(BF)


def vmem():
    return pl.BlockSpec(memory_space=pltpu.VMEM)


def smem():
    return pl.BlockSpec(memory_space=pltpu.SMEM)


def anywhere():
    return pl.BlockSpec(memory_space=pl.ANY)


def per_device(
    queries, keys, values, forward_out, grad_out, out_weight,
    block_docs, doc_group, prefix_keys, prefix_values,
):
    me = lax.axis_index("ctx").astype(jnp.int32).reshape(1)
    head = lax.axis_index("head").astype(jnp.int32).reshape(1)

    own = jnp.concatenate([keys[:, 0], prefix_keys[:, 0], values[:, 0], prefix_values[:, 0]])
    beside = swap_ctx(own, z_swap)
    up = from_head(grad_out, 1, 0)
    down = from_head(grad_out, -1, 0)
    over = from_head(grad_out, 0, 1)
    pair = jnp.stack([own, beside])
    from_next = swap_ctx(pair, x_shift(-1))
    from_prev = swap_ctx(pair, x_shift(1))
    from_far = swap_ctx(pair, x_shift(2))
    over_up = from_head(up, 0, 1)
    over_down = from_head(over, -1, 0)
    far = from_head(up, 1, 0)
    over_far = from_head(over_up, 1, 0)
    from_next, from_prev, from_far, down, over_up, over_down, far, over_far = lax.optimization_barrier(
        (from_next, from_prev, from_far, down, over_up, over_down, far, over_far)
    )
    same = jnp.stack([pair, from_next, from_far, from_prev])
    other = swap_ctx(same, core_swap)

    part = jax.ShapeDtypeStruct((8, 2 * PIECE, HD), BF)
    dq, keep, send = pl.pallas_call(
        main_kernel,
        out_shape=(jax.ShapeDtypeStruct((ROWS, HD), BF), part, part),
        in_specs=[smem()] * 4 + [anywhere()] * 9 + [vmem()] * 4,
        out_specs=(vmem(),) * 3,
        scratch_shapes=[
            pltpu.VMEM((HALF, 8 * DLOC), BF),
            pltpu.VMEM((CHUNK, 8 * DLOC), BF),
            pltpu.SemaphoreType.DMA((16,)),
            pltpu.VMEM((CHUNK, 8, HD), F32),
            pltpu.VMEM((ROWS, HD), BF),
            pltpu.VMEM((1, ROWS), F32),
            pltpu.VMEM((1, ROWS), F32),
            pltpu.VMEM((8, ROWS), F32),
            pltpu.VMEM((8, ROWS), F32),
            pltpu.VMEM((TOKENS, HD), BF),
            pltpu.VMEM((PTOK, HD), BF),
            pltpu.VMEM((TOKENS, HD), BF),
            pltpu.VMEM((PTOK, HD), BF),
            pltpu.VMEM((TOKENS, HD), F32),
            pltpu.VMEM((TOKENS, HD), F32),
            pltpu.VMEM((PTOK, HD), F32),
            pltpu.VMEM((PTOK, HD), F32),
            pltpu.VMEM((HD, ROWS), F32),
        ],
        compiler_params=pltpu.CompilerParams(vmem_limit_bytes=56 * 1024 * 1024),
        cost_estimate=pl.CostEstimate(flops=10**10, bytes_accessed=10**7, transcendentals=10**7),
        name="attention_grads",
    )(
        me, head, block_docs, doc_group, grad_out, up, down, over, over_up, over_down, far, over_far,
        out_weight, queries.reshape(ROWS, HD), forward_out.reshape(ROWS, HD), same, other,
    )

    got = swap_ctx(send, core_swap)
    both = (keep.astype(F32) + got.astype(F32)).astype(BF)
    terms = lax.all_to_all(
        both, "ctx", 0, 0, axis_index_groups=[[i for i in range(16) if i % 2 == c] for c in range(2)]
    )
    packed = jax.ShapeDtypeStruct((CHUNK, HD), BF)
    prompt = jax.ShapeDtypeStruct((PCHUNK, HD), BF)
    outs = pl.pallas_call(
        sum_kernel,
        out_shape=(packed, packed, prompt, prompt),
        in_specs=[vmem()],
        out_specs=(vmem(),) * 4,
        name="last_sum",
    )(terms)
    return (dq.reshape(CHUNK, 8, HD), *(out[:, None] for out in outs))


def solution(mesh):
    tokens = P("ctx", "head", None)
    in_specs = (
        tokens, tokens, tokens, tokens, P("ctx", "head"), P("head", None), P(), P(), tokens, tokens,
    )
    return jax.shard_map(
        per_device, mesh=mesh, in_specs=in_specs, out_specs=(tokens,) * 5, check_vma=False
    )
```

```python
import jax
import jax.numpy as jnp
from jax import lax
from jax.experimental import pallas as pl
from jax.experimental.pallas import tpu as pltpu
from jax.sharding import PartitionSpec as P

BLK = 128
NBLK = 32
NDOCS = 8
HD = 128
CHUNK = 256
PCHUNK = 64
ROWS = 2048
HALF = 1024
TOKENS = 4096
PTOK = 1024
PLEN = 256
DLOC = 640
PIECE = CHUNK + PCHUNK

FACTOR = HD ** -0.5
LOG2E = 1.4426950408889634
SCALE2 = FACTOR * LOG2E
NEGATIVE = -1e30

BF = jnp.bfloat16
F32 = jnp.float32


def dot(a, b, ca, cb):
    return lax.dot_general(a, b, (((ca,), (cb,)), ((), ())), preferred_element_type=F32)


def swap_ctx(value, move):
    return lax.ppermute(value, "ctx", [(i, move(i)) for i in range(16)])


def head_of(head, dy, dz):
    return ((head // 2 + dy) % 4) * 2 + (head % 2 + dz) % 2


def from_head(value, dy, dz):
    return lax.ppermute(value, "head", [(head_of(i, dy, dz), i) for i in range(8)])


def x_shift(steps):
    return lambda i: ((i // 4 + steps) % 4) * 4 + i % 4


def core_swap(i):
    return i ^ 1


def z_swap(i):
    return i ^ 2


def ctx_of(me, s, i, other):
    x = (me // 4 + s) % 4
    z = (me // 2) % 2
    core = me % 2
    z = 1 - z if i else z
    core = 1 - core if other else core
    return x * 4 + z * 2 + core


def spread(me, pieces, places, sems):
    copies = []
    for p, piece in enumerate(pieces):
        for i in range(2):
            at = ctx_of(me, p % 4, i, p // 4)
            first = 0
            for n, place in enumerate(places):
                size = CHUNK if n % 2 == 0 else PCHUNK
                copies.append(
                    pltpu.make_async_copy(
                        piece.at[i, first : first + size],
                        place.at[pl.ds(pl.multiple_of(at * size, size), size)],
                        sems.at[len(copies)],
                    )
                )
                first += size
    return copies


def block_facts(docs, groups, block):
    doc = docs[block]
    start = jnp.int32(0)
    for j in range(NBLK):
        start = start + (docs[j] < doc).astype(jnp.int32)
    return start, groups[doc]


def own_tokens(alike):
    keys = lax.broadcasted_iota(jnp.int32, (CHUNK, ROWS), 0)
    toks = lax.broadcasted_iota(jnp.int32, (CHUNK, ROWS), 1) >> 3
    first = jnp.where(alike, 0, toks >> 7 << 7)
    return (keys <= toks) & (keys >= first)


def rows_at(first, count):
    return pl.ds(pl.multiple_of(first, BLK), count)


PLACES = ((0, 0), (1, 0), (-1, 0), (0, 1), (1, 1), (-1, 1), (2, 0), (2, 1))


BOTH = slice(0, ROWS)
HALVES = (slice(0, HALF), slice(HALF, ROWS))


AHEAD = 23
SPAN = PLEN + CHUNK + AHEAD * BLK
PAIRS_AT = 2 + AHEAD // 4
SLOTS = PAIRS_AT + AHEAD // 2 + 1


def walk(me, docs, groups, prompt, packed):
    start, group = block_facts(docs, groups, 2 * me)
    other_start, other_group = block_facts(docs, groups, 2 * me + 1)
    alike = docs[2 * me] == docs[2 * me + 1]
    kept = pl.ds(0, PLEN)
    prompt(HALVES[0], rows_at(group * PLEN, PLEN), kept, 0, None)
    prompt(HALVES[1], rows_at(other_group * PLEN, PLEN), kept, 0, None)
    own = pl.ds(pl.multiple_of(me * CHUNK, CHUNK), CHUNK)
    packed(BOTH, own, pl.ds(PLEN, CHUNK), 1, alike)
    count = 2 * me - start
    fours = count // 4
    for columns, wanted, steps in (
        (
            BOTH,
            alike,
            ((4, 0, fours, 2), (2, 4 * fours, count // 2 % 2, PAIRS_AT), (1, count - 1, count % 2, SLOTS - 1)),
        ),
        (
            HALVES[0],
            jnp.logical_not(alike),
            ((2, 0, count // 2, PAIRS_AT), (1, count - 1, count % 2, SLOTS - 1)),
        ),
    ):
        for size, offset, trips, slot in steps:

            def step(i, carry):
                at = offset + size * i
                rows = rows_at((start + at) * BLK, size * BLK)
                packed(columns, rows, rows_at(PLEN + CHUNK + at * BLK, size * BLK), slot + i, None)
                return carry

            lax.fori_loop(0, jnp.where(wanted, trips, 0), step, 0)


def main_kernel(me_ref, head_ref, docs, groups, *refs):
    pieces, parts = refs[:9], refs[9:17]
    (weight, q_ref, o_ref, dq_ref, keep_ref, send_ref,
     held, grads, sems, part_sems, g3, g_ref, delta_ref, lse_ref, tops, totals, weights,
     kall, pkall, vall, pvall, dk, dv, dpk, dpv, dq_acc) = refs[17:]
    me = me_ref[0]
    spreads = spread(me, parts, (kall, pkall, vall, pvall), part_sems)
    key_copies = [copy for n, copy in enumerate(spreads) if n % 4 < 2]
    copies = [copy for n, copy in enumerate(spreads) if n % 4 >= 2]
    for k, place in enumerate(PLACES):
        source = pl.multiple_of(head_of(head_ref[0], *place) * DLOC, 128)
        at = pl.ds(k * DLOC, DLOC)
        copies.append(
            pltpu.make_async_copy(weight.at[:, pl.ds(source, DLOC)], held.at[:, at], sems.at[k])
        )
        if k < 7:
            copies.append(pltpu.make_async_copy(pieces[k], grads.at[:, at], sems.at[8 + k]))
    for half in range(2):
        copies.append(
            pltpu.make_async_copy(
                pieces[7 + half],
                grads.at[half * BLK : (half + 1) * BLK, 7 * DLOC :],
                sems.at[15 + half],
            )
        )
    for copy in key_copies + copies:
        copy.start()
    for ref in (dk, dv, dpk, dpv, dq_acc):
        ref[...] = jnp.zeros_like(ref)
    for copy in key_copies:
        copy.wait()

    def sums(keys_ref, columns, rows, kept, slot, alike, fresh):
        score = dot(keys_ref[rows, :], q_ref[columns, :], 1, 1) * SCALE2
        if alike is not None:
            score = jnp.where(own_tokens(alike), score, NEGATIVE)
        shape = score.shape
        score = score.reshape(shape[0] // 8, 8, shape[1])
        new = jnp.max(score, axis=0)
        if not fresh:
            top = tops[SLOTS, :, columns]
            new = jnp.maximum(top, new)
        part = jnp.exp2(score - new[None])
        total = jnp.sum(part, axis=0)
        if not fresh:
            total = total + totals[:, columns] * jnp.exp2(top - new)
        weights[kept, columns] = part.reshape(shape).astype(BF)
        totals[:, columns] = total
        tops[slot, :, columns] = new
        tops[SLOTS, :, columns] = new

    def prompt_sums(columns, rows, kept, slot, alike):
        sums(pkall, columns, rows, kept, slot, alike, True)

    def packed_sums(columns, rows, kept, slot, alike):
        sums(kall, columns, rows, kept, slot, alike, False)

    walk(me, docs, groups, prompt_sums, packed_sums)
    top = tops[SLOTS]
    best = jnp.max(top, axis=0, keepdims=True)
    whole = jnp.sum(totals[...] * jnp.exp2(top - best), axis=0, keepdims=True)
    lse_ref[...] = best + jnp.log2(whole)

    for copy in copies:
        copy.wait()
    total = dot(grads[...], held[...], 1, 1)
    for h in range(8):
        g3[:, h, :] = total[:, h * HD : (h + 1) * HD]
    for half, at in enumerate(HALVES):
        low = g3[half * BLK : (half + 1) * BLK].reshape(HALF, HD).astype(BF)
        g_ref[at, :] = low
        product = low.astype(F32) * o_ref[at, :].astype(F32)
        delta_ref[:, at] = jnp.sum(product.T, axis=0, keepdims=True)

    def grads_of(keys_ref, vals_ref, dk_ref, dv_ref, columns, rows, kept, slot):
        g = g_ref[columns, :]
        keys = keys_ref[rows, :]
        dprob = dot(vals_ref[rows, :], g, 1, 1)
        share = jnp.exp2(tops[slot, :, columns] - lse_ref[:, columns])
        part = weights[kept, columns].astype(F32)
        shape = part.shape
        prob = (part.reshape(shape[0] // 8, 8, shape[1]) * share[None]).reshape(shape)
        dscore = (prob * (dprob - delta_ref[:, columns])).astype(BF)
        dv_ref[rows, :] += dot(prob.astype(BF), g, 1, 0)
        dk_ref[rows, :] += dot(dscore, q_ref[columns, :], 1, 0)
        dq_acc[:, columns] += dot(keys.T, dscore, 1, 0)

    def prompt_grads(columns, rows, kept, slot, alike):
        grads_of(pkall, pvall, dpk, dpv, columns, rows, kept, slot)

    def packed_grads(columns, rows, kept, slot, alike):
        grads_of(kall, vall, dk, dv, columns, rows, kept, slot)

    walk(me, docs, groups, prompt_grads, packed_grads)
    for at in HALVES:
        dq_ref[at, :] = (dq_acc[:, at].T * FACTOR).astype(BF)

    core = me % 2
    for which, ref in ((core, keep_ref), (1 - core, send_ref)):
        for j in range(8):
            to = 2 * j + which
            big = pl.ds(pl.multiple_of(to * CHUNK, CHUNK), CHUNK)
            small = pl.ds(pl.multiple_of(to * PCHUNK, PCHUNK), PCHUNK)
            ref[j, :CHUNK, :] = dk[big, :].astype(BF)
            ref[j, CHUNK:PIECE, :] = dpk[small, :].astype(BF)
            ref[j, PIECE : PIECE + CHUNK, :] = dv[big, :].astype(BF)
            ref[j, PIECE + CHUNK :, :] = dpv[small, :].astype(BF)


def sum_kernel(terms, k_ref, v_ref, pk_ref, pv_ref):
    total = terms[0].astype(F32)
    for j in range(1, 8):
        total = total + terms[j].astype(F32)
    k_ref[...] = (total[:CHUNK] * FACTOR).astype(BF)
    pk_ref[...] = (total[CHUNK:PIECE] * FACTOR).astype(BF)
    v_ref[...] = total[PIECE : PIECE + CHUNK].astype(BF)
    pv_ref[...] = total[PIECE + CHUNK :].astype(BF)


def vmem():
    return pl.BlockSpec(memory_space=pltpu.VMEM)


def smem():
    return pl.BlockSpec(memory_space=pltpu.SMEM)


def anywhere():
    return pl.BlockSpec(memory_space=pl.ANY)


def per_device(
    queries, keys, values, forward_out, grad_out, out_weight,
    block_docs, doc_group, prefix_keys, prefix_values,
):
    me = lax.axis_index("ctx").astype(jnp.int32).reshape(1)
    head = lax.axis_index("head").astype(jnp.int32).reshape(1)

    own = jnp.concatenate([keys[:, 0], prefix_keys[:, 0], values[:, 0], prefix_values[:, 0]])
    beside = swap_ctx(own, z_swap)
    up = from_head(grad_out, 1, 0)
    down = from_head(grad_out, -1, 0)
    over = from_head(grad_out, 0, 1)
    pair = jnp.stack([own, beside])
    from_next = swap_ctx(pair, x_shift(-1))
    from_prev = swap_ctx(pair, x_shift(1))
    from_far = swap_ctx(pair, x_shift(2))
    over_up = from_head(up, 0, 1)
    over_down = from_head(over, -1, 0)
    far = from_head(up, 1, 0)
    down, over_up, over_down, far = lax.optimization_barrier((down, over_up, over_down, far))
    over_far0 = from_head(over_up[:BLK], 1, 0)
    over_far1 = from_head(over_down[BLK:], -1, 0)
    same = (pair, from_next, from_far, from_prev)
    other = tuple(swap_ctx(piece, core_swap) for piece in same)

    part = jax.ShapeDtypeStruct((8, 2 * PIECE, HD), BF)
    dq, keep, send = pl.pallas_call(
        main_kernel,
        out_shape=(jax.ShapeDtypeStruct((ROWS, HD), BF), part, part),
        in_specs=[smem()] * 4 + [anywhere()] * 18 + [vmem()] * 2,
        out_specs=(vmem(),) * 3,
        scratch_shapes=[
            pltpu.VMEM((HALF, 8 * DLOC), BF),
            pltpu.VMEM((CHUNK, 8 * DLOC), BF),
            pltpu.SemaphoreType.DMA((17,)),
            pltpu.SemaphoreType.DMA((64,)),
            pltpu.VMEM((CHUNK, 8, HD), F32),
            pltpu.VMEM((ROWS, HD), BF),
            pltpu.VMEM((1, ROWS), F32),
            pltpu.VMEM((1, ROWS), F32),
            pltpu.VMEM((SLOTS + 1, 8, ROWS), F32),
            pltpu.VMEM((8, ROWS), F32),
            pltpu.VMEM((SPAN, ROWS), BF),
            pltpu.VMEM((TOKENS, HD), BF),
            pltpu.VMEM((PTOK, HD), BF),
            pltpu.VMEM((TOKENS, HD), BF),
            pltpu.VMEM((PTOK, HD), BF),
            pltpu.VMEM((TOKENS, HD), F32),
            pltpu.VMEM((TOKENS, HD), F32),
            pltpu.VMEM((PTOK, HD), F32),
            pltpu.VMEM((PTOK, HD), F32),
            pltpu.VMEM((HD, ROWS), F32),
        ],
        compiler_params=pltpu.CompilerParams(vmem_limit_bytes=60 * 1024 * 1024),
        cost_estimate=pl.CostEstimate(flops=10**10, bytes_accessed=10**7, transcendentals=10**7),
        name="attention_grads",
    )(
        me, head, block_docs, doc_group, grad_out, up, down, over, over_up, over_down, far,
        over_far0, over_far1, *same, *other,
        out_weight, queries.reshape(ROWS, HD), forward_out.reshape(ROWS, HD),
    )

    got = swap_ctx(send, core_swap)
    both = (keep.astype(F32) + got.astype(F32)).astype(BF)
    terms = lax.all_to_all(
        both, "ctx", 0, 0, axis_index_groups=[[i for i in range(16) if i % 2 == c] for c in range(2)]
    )
    packed = jax.ShapeDtypeStruct((CHUNK, HD), BF)
    prompt = jax.ShapeDtypeStruct((PCHUNK, HD), BF)
    outs = pl.pallas_call(
        sum_kernel,
        out_shape=(packed, packed, prompt, prompt),
        in_specs=[vmem()],
        out_specs=(vmem(),) * 4,
        name="last_sum",
    )(terms)
    return (dq.reshape(CHUNK, 8, HD), *(out[:, None] for out in outs))


def solution(mesh):
    tokens = P("ctx", "head", None)
    in_specs = (
        tokens, tokens, tokens, tokens, P("ctx", "head"), P("head", None), P(), P(), tokens, tokens,
    )
    return jax.shard_map(
        per_device, mesh=mesh, in_specs=in_specs, out_specs=(tokens,) * 5, check_vma=False
    )
```

```python
import jax
import jax.numpy as jnp
from jax import lax
from jax.experimental import pallas as pl
from jax.experimental.pallas import tpu as pltpu
from jax.sharding import PartitionSpec as P

BLK = 128
NBLK = 32
NDOCS = 8
HD = 128
CHUNK = 256
PCHUNK = 64
ROWS = 2048
HALF = 1024
TOKENS = 4096
PTOK = 1024
PLEN = 256
DLOC = 640
PIECE = CHUNK + PCHUNK

FACTOR = HD ** -0.5
LOG2E = 1.4426950408889634
SCALE2 = FACTOR * LOG2E
NEGATIVE = -1e30

BF = jnp.bfloat16
F32 = jnp.float32


def dot(a, b, ca, cb):
    return lax.dot_general(a, b, (((ca,), (cb,)), ((), ())), preferred_element_type=F32)


def swap_ctx(value, move):
    return lax.ppermute(value, "ctx", [(i, move(i)) for i in range(16)])


def head_of(head, dy, dz):
    return ((head // 2 + dy) % 4) * 2 + (head % 2 + dz) % 2


def from_head(value, dy, dz):
    return lax.ppermute(value, "head", [(head_of(i, dy, dz), i) for i in range(8)])


def x_shift(steps):
    return lambda i: ((i // 4 + steps) % 4) * 4 + i % 4


def core_swap(i):
    return i ^ 1


def z_swap(i):
    return i ^ 2


def ctx_of(me, s, i, other):
    x = (me // 4 + s) % 4
    z = (me // 2) % 2
    core = me % 2
    z = 1 - z if i else z
    core = 1 - core if other else core
    return x * 4 + z * 2 + core


def spread(me, pieces, places, sems):
    copies = []
    for p, piece in enumerate(pieces):
        for i in range(2):
            at = ctx_of(me, p % 4, i, p // 4)
            first = 0
            for n, place in enumerate(places):
                size = CHUNK if n % 2 == 0 else PCHUNK
                copies.append(
                    pltpu.make_async_copy(
                        piece.at[i, first : first + size],
                        place.at[pl.ds(pl.multiple_of(at * size, size), size)],
                        sems.at[len(copies)],
                    )
                )
                first += size
    return copies


def block_facts(docs, groups, block):
    doc = docs[block]
    start = jnp.int32(0)
    for j in range(NBLK):
        start = start + (docs[j] < doc).astype(jnp.int32)
    return start, groups[doc]


def own_tokens(alike):
    keys = lax.broadcasted_iota(jnp.int32, (CHUNK, ROWS), 0)
    toks = lax.broadcasted_iota(jnp.int32, (CHUNK, ROWS), 1) >> 3
    first = jnp.where(alike, 0, toks >> 7 << 7)
    return (keys <= toks) & (keys >= first)


def rows_at(first, count):
    return pl.ds(pl.multiple_of(first, BLK), count)


PLACES = ((0, 0), (1, 0), (-1, 0), (0, 1), (1, 1), (-1, 1), (2, 0), (2, 1))


BOTH = slice(0, ROWS)
HALVES = (slice(0, HALF), slice(HALF, ROWS))


AHEAD = 23
SPAN = PLEN + CHUNK + AHEAD * BLK
PAIRS_AT = 2 + AHEAD // 4
SLOTS = PAIRS_AT + AHEAD // 2 + 1


def walk(me, docs, groups, prompt, packed):
    start, group = block_facts(docs, groups, 2 * me)
    other_start, other_group = block_facts(docs, groups, 2 * me + 1)
    alike = docs[2 * me] == docs[2 * me + 1]
    kept = pl.ds(0, PLEN)
    prompt(HALVES[0], rows_at(group * PLEN, PLEN), kept, 0, None)
    prompt(HALVES[1], rows_at(other_group * PLEN, PLEN), kept, 0, None)
    own = pl.ds(pl.multiple_of(me * CHUNK, CHUNK), CHUNK)
    packed(BOTH, own, pl.ds(PLEN, CHUNK), 1, alike)
    count = 2 * me - start
    fours = count // 4
    for columns, wanted, steps in (
        (
            BOTH,
            alike,
            ((4, 0, fours, 2), (2, 4 * fours, count // 2 % 2, PAIRS_AT), (1, count - 1, count % 2, SLOTS - 1)),
        ),
        (
            HALVES[0],
            jnp.logical_not(alike),
            ((2, 0, count // 2, PAIRS_AT), (1, count - 1, count % 2, SLOTS - 1)),
        ),
    ):
        for size, offset, trips, slot in steps:

            def step(i, carry):
                at = offset + size * i
                rows = rows_at((start + at) * BLK, size * BLK)
                packed(columns, rows, rows_at(PLEN + CHUNK + at * BLK, size * BLK), slot + i, None)
                return carry

            lax.fori_loop(0, jnp.where(wanted, trips, 0), step, 0)


def main_kernel(me_ref, head_ref, docs, groups, *refs):
    pieces, parts = refs[:9], refs[9:17]
    (weight, forward, q_ref, dq_ref, keep_ref, send_ref,
     held, grads, sems, part_sems, g3, g_ref, delta_ref, lse_ref, tops, totals, weights,
     kall, pkall, vall, pvall, dk, dv, dpk, dpv, dq_acc, o_ref) = refs[17:]
    me = me_ref[0]
    spreads = spread(me, parts, (kall, pkall, vall, pvall), part_sems)
    key_copies = [copy for n, copy in enumerate(spreads) if n % 4 < 2]
    copies = [copy for n, copy in enumerate(spreads) if n % 4 >= 2]
    for k, place in enumerate(PLACES):
        source = pl.multiple_of(head_of(head_ref[0], *place) * DLOC, 128)
        at = pl.ds(k * DLOC, DLOC)
        copies.append(
            pltpu.make_async_copy(weight.at[:, pl.ds(source, DLOC)], held.at[:, at], sems.at[k])
        )
        if k < 7:
            copies.append(pltpu.make_async_copy(pieces[k], grads.at[:, at], sems.at[8 + k]))
    for half in range(2):
        copies.append(
            pltpu.make_async_copy(
                pieces[7 + half],
                grads.at[half * BLK : (half + 1) * BLK, 7 * DLOC :],
                sems.at[15 + half],
            )
        )
    copies.append(pltpu.make_async_copy(forward, o_ref, sems.at[17]))
    for copy in key_copies + copies:
        copy.start()
    for ref in (dk, dv, dpk, dpv, dq_acc):
        ref[...] = jnp.zeros_like(ref)
    for copy in key_copies:
        copy.wait()

    def sums(keys_ref, columns, rows, kept, slot, alike, fresh):
        score = dot(keys_ref[rows, :], q_ref[columns, :], 1, 1) * SCALE2
        if alike is not None:
            score = jnp.where(own_tokens(alike), score, NEGATIVE)
        shape = score.shape
        score = score.reshape(shape[0] // 8, 8, shape[1])
        new = jnp.max(score, axis=0)
        if not fresh:
            top = tops[SLOTS, :, columns]
            new = jnp.maximum(top, new)
        part = jnp.exp2(score - new[None])
        total = jnp.sum(part, axis=0)
        if not fresh:
            total = total + totals[:, columns] * jnp.exp2(top - new)
        weights[kept, columns] = part.reshape(shape).astype(BF)
        totals[:, columns] = total
        tops[slot, :, columns] = new
        tops[SLOTS, :, columns] = new

    def prompt_sums(columns, rows, kept, slot, alike):
        sums(pkall, columns, rows, kept, slot, alike, True)

    def packed_sums(columns, rows, kept, slot, alike):
        sums(kall, columns, rows, kept, slot, alike, False)

    walk(me, docs, groups, prompt_sums, packed_sums)
    top = tops[SLOTS]
    best = jnp.max(top, axis=0, keepdims=True)
    whole = jnp.sum(totals[...] * jnp.exp2(top - best), axis=0, keepdims=True)
    lse_ref[...] = best + jnp.log2(whole)

    for copy in copies:
        copy.wait()
    total = dot(grads[...], held[...], 1, 1)
    for h in range(8):
        g3[:, h, :] = total[:, h * HD : (h + 1) * HD]
    for half, at in enumerate(HALVES):
        low = g3[half * BLK : (half + 1) * BLK].reshape(HALF, HD).astype(BF)
        g_ref[at, :] = low
        product = low.astype(F32) * o_ref[at, :].astype(F32)
        delta_ref[:, at] = jnp.sum(product.T, axis=0, keepdims=True)

    def grads_of(keys_ref, vals_ref, dk_ref, dv_ref, columns, rows, kept, slot):
        g = g_ref[columns, :]
        keys = keys_ref[rows, :]
        dprob = dot(vals_ref[rows, :], g, 1, 1)
        share = jnp.exp2(tops[slot, :, columns] - lse_ref[:, columns])
        part = weights[kept, columns].astype(F32)
        shape = part.shape
        prob = (part.reshape(shape[0] // 8, 8, shape[1]) * share[None]).reshape(shape)
        low = prob.astype(BF)
        dscore = low * (dprob - delta_ref[:, columns]).astype(BF)
        dv_ref[rows, :] += dot(low, g, 1, 0)
        dk_ref[rows, :] += dot(dscore, q_ref[columns, :], 1, 0)
        dq_acc[:, columns] += dot(keys.T, dscore, 1, 0)

    def prompt_grads(columns, rows, kept, slot, alike):
        grads_of(pkall, pvall, dpk, dpv, columns, rows, kept, slot)

    def packed_grads(columns, rows, kept, slot, alike):
        grads_of(kall, vall, dk, dv, columns, rows, kept, slot)

    walk(me, docs, groups, prompt_grads, packed_grads)
    for at in HALVES:
        dq_ref[at, :] = (dq_acc[:, at].T * FACTOR).astype(BF)

    core = me % 2
    for which, ref in ((core, keep_ref), (1 - core, send_ref)):
        for j in range(8):
            to = 2 * j + which
            big = pl.ds(pl.multiple_of(to * CHUNK, CHUNK), CHUNK)
            small = pl.ds(pl.multiple_of(to * PCHUNK, PCHUNK), PCHUNK)
            ref[j, :CHUNK, :] = dk[big, :].astype(BF)
            ref[j, CHUNK:PIECE, :] = dpk[small, :].astype(BF)
            ref[j, PIECE : PIECE + CHUNK, :] = dv[big, :].astype(BF)
            ref[j, PIECE + CHUNK :, :] = dpv[small, :].astype(BF)


def sum_kernel(terms, k_ref, v_ref, pk_ref, pv_ref):
    total = terms[0].astype(F32)
    for j in range(1, 8):
        total = total + terms[j].astype(F32)
    k_ref[...] = (total[:CHUNK] * FACTOR).astype(BF)
    pk_ref[...] = (total[CHUNK:PIECE] * FACTOR).astype(BF)
    v_ref[...] = total[PIECE : PIECE + CHUNK].astype(BF)
    pv_ref[...] = total[PIECE + CHUNK :].astype(BF)


def vmem():
    return pl.BlockSpec(memory_space=pltpu.VMEM)


def smem():
    return pl.BlockSpec(memory_space=pltpu.SMEM)


def anywhere():
    return pl.BlockSpec(memory_space=pl.ANY)


def per_device(
    queries, keys, values, forward_out, grad_out, out_weight,
    block_docs, doc_group, prefix_keys, prefix_values,
):
    me = lax.axis_index("ctx").astype(jnp.int32).reshape(1)
    head = lax.axis_index("head").astype(jnp.int32).reshape(1)

    own = jnp.concatenate([keys[:, 0], prefix_keys[:, 0], values[:, 0], prefix_values[:, 0]])
    beside = swap_ctx(own, z_swap)
    up = from_head(grad_out, 1, 0)
    down = from_head(grad_out, -1, 0)
    over = from_head(grad_out, 0, 1)
    pair = jnp.stack([own, beside])
    from_next = swap_ctx(pair, x_shift(-1))
    from_prev = swap_ctx(pair, x_shift(1))
    from_far = swap_ctx(pair, x_shift(2))
    over_up = from_head(up, 0, 1)
    over_down = from_head(over, -1, 0)
    far = from_head(up, 1, 0)
    down, over_up, over_down, far = lax.optimization_barrier((down, over_up, over_down, far))
    over_far0 = from_head(over_up[:BLK], 1, 0)
    over_far1 = from_head(over_down[BLK:], -1, 0)
    same = (pair, from_next, from_far, from_prev)
    other = tuple(swap_ctx(piece, core_swap) for piece in same)

    part = jax.ShapeDtypeStruct((8, 2 * PIECE, HD), BF)
    dq, keep, send = pl.pallas_call(
        main_kernel,
        out_shape=(jax.ShapeDtypeStruct((ROWS, HD), BF), part, part),
        in_specs=[smem()] * 4 + [anywhere()] * 19 + [vmem()],
        out_specs=(vmem(),) * 3,
        scratch_shapes=[
            pltpu.VMEM((HALF, 8 * DLOC), BF),
            pltpu.VMEM((CHUNK, 8 * DLOC), BF),
            pltpu.SemaphoreType.DMA((18,)),
            pltpu.SemaphoreType.DMA((64,)),
            pltpu.VMEM((CHUNK, 8, HD), F32),
            pltpu.VMEM((ROWS, HD), BF),
            pltpu.VMEM((1, ROWS), F32),
            pltpu.VMEM((1, ROWS), F32),
            pltpu.VMEM((SLOTS + 1, 8, ROWS), F32),
            pltpu.VMEM((8, ROWS), F32),
            pltpu.VMEM((SPAN, ROWS), BF),
            pltpu.VMEM((TOKENS, HD), BF),
            pltpu.VMEM((PTOK, HD), BF),
            pltpu.VMEM((TOKENS, HD), BF),
            pltpu.VMEM((PTOK, HD), BF),
            pltpu.VMEM((TOKENS, HD), F32),
            pltpu.VMEM((TOKENS, HD), F32),
            pltpu.VMEM((PTOK, HD), F32),
            pltpu.VMEM((PTOK, HD), F32),
            pltpu.VMEM((HD, ROWS), F32),
            pltpu.VMEM((ROWS, HD), BF),
        ],
        compiler_params=pltpu.CompilerParams(vmem_limit_bytes=60 * 1024 * 1024),
        cost_estimate=pl.CostEstimate(flops=10**10, bytes_accessed=10**7, transcendentals=10**7),
        name="attention_grads",
    )(
        me, head, block_docs, doc_group, grad_out, up, down, over, over_up, over_down, far,
        over_far0, over_far1, *same, *other,
        out_weight, forward_out.reshape(ROWS, HD), queries.reshape(ROWS, HD),
    )

    got = swap_ctx(send, core_swap)
    both = (keep.astype(F32) + got.astype(F32)).astype(BF)
    terms = lax.all_to_all(
        both, "ctx", 0, 0, axis_index_groups=[[i for i in range(16) if i % 2 == c] for c in range(2)]
    )
    packed = jax.ShapeDtypeStruct((CHUNK, HD), BF)
    prompt = jax.ShapeDtypeStruct((PCHUNK, HD), BF)
    outs = pl.pallas_call(
        sum_kernel,
        out_shape=(packed, packed, prompt, prompt),
        in_specs=[vmem()],
        out_specs=(vmem(),) * 4,
        name="last_sum",
    )(terms)
    return (dq.reshape(CHUNK, 8, HD), *(out[:, None] for out in outs))


def solution(mesh):
    tokens = P("ctx", "head", None)
    in_specs = (
        tokens, tokens, tokens, tokens, P("ctx", "head"), P("head", None), P(), P(), tokens, tokens,
    )
    return jax.shard_map(
        per_device, mesh=mesh, in_specs=in_specs, out_specs=(tokens,) * 5, check_vma=False
    )
```

```python
import jax
import jax.numpy as jnp
from jax import lax
from jax.experimental import pallas as pl
from jax.experimental.pallas import tpu as pltpu
from jax.sharding import PartitionSpec as P

BLK = 128
NBLK = 32
NDOCS = 8
HD = 128
CHUNK = 256
PCHUNK = 64
ROWS = 2048
HALF = 1024
TOKENS = 4096
PTOK = 1024
PLEN = 256
DLOC = 640
PIECE = CHUNK + PCHUNK

FACTOR = HD ** -0.5
LOG2E = 1.4426950408889634
SCALE2 = FACTOR * LOG2E
NEGATIVE = -1e30

BF = jnp.bfloat16
F32 = jnp.float32


def dot(a, b, ca, cb):
    return lax.dot_general(a, b, (((ca,), (cb,)), ((), ())), preferred_element_type=F32)


def swap_ctx(value, move):
    return lax.ppermute(value, "ctx", [(i, move(i)) for i in range(16)])


def head_of(head, dy, dz):
    return ((head // 2 + dy) % 4) * 2 + (head % 2 + dz) % 2


def from_head(value, dy, dz):
    return lax.ppermute(value, "head", [(head_of(i, dy, dz), i) for i in range(8)])


def x_shift(steps):
    return lambda i: ((i // 4 + steps) % 4) * 4 + i % 4


def core_swap(i):
    return i ^ 1


def z_swap(i):
    return i ^ 2


def ctx_of(me, s, i, other):
    x = (me // 4 + s) % 4
    z = (me // 2) % 2
    core = me % 2
    z = 1 - z if i else z
    core = 1 - core if other else core
    return x * 4 + z * 2 + core


def spread(me, pieces, places, sems):
    copies = []
    for p, piece in enumerate(pieces):
        for i in range(2):
            at = ctx_of(me, p % 4, i, p // 4)
            first = 0
            for n, place in enumerate(places):
                size = CHUNK if n % 2 == 0 else PCHUNK
                copies.append(
                    pltpu.make_async_copy(
                        piece.at[i, first : first + size],
                        place.at[pl.ds(pl.multiple_of(at * size, size), size)],
                        sems.at[len(copies)],
                    )
                )
                first += size
    return copies


def block_facts(docs, groups, block):
    doc = docs[block]
    start = jnp.int32(0)
    for j in range(NBLK):
        start = start + (docs[j] < doc).astype(jnp.int32)
    return start, groups[doc]


def own_tokens(alike):
    keys = lax.broadcasted_iota(jnp.int32, (CHUNK, ROWS), 0)
    toks = lax.broadcasted_iota(jnp.int32, (CHUNK, ROWS), 1) >> 3
    first = jnp.where(alike, 0, toks >> 7 << 7)
    return (keys <= toks) & (keys >= first)


def rows_at(first, count):
    return pl.ds(pl.multiple_of(first, BLK), count)


PLACES = ((0, 0), (1, 0), (-1, 0), (0, 1), (1, 1), (-1, 1), (2, 0), (2, 1))


BOTH = slice(0, ROWS)
HALVES = (slice(0, HALF), slice(HALF, ROWS))


AHEAD = 23
SPAN = PLEN + CHUNK + AHEAD * BLK
PAIRS_AT = 2 + AHEAD // 4
SLOTS = PAIRS_AT + AHEAD // 2 + 1


def walk(me, docs, groups, prompt, packed):
    start, group = block_facts(docs, groups, 2 * me)
    other_start, other_group = block_facts(docs, groups, 2 * me + 1)
    alike = docs[2 * me] == docs[2 * me + 1]
    kept = pl.ds(0, PLEN)
    prompt(HALVES[0], rows_at(group * PLEN, PLEN), kept, 0, None)
    prompt(HALVES[1], rows_at(other_group * PLEN, PLEN), kept, 0, None)
    own = pl.ds(pl.multiple_of(me * CHUNK, CHUNK), CHUNK)
    packed(BOTH, own, pl.ds(PLEN, CHUNK), 1, alike)
    count = 2 * me - start
    fours = count // 4
    for columns, wanted, steps in (
        (
            BOTH,
            alike,
            ((4, 0, fours, 2), (2, 4 * fours, count // 2 % 2, PAIRS_AT), (1, count - 1, count % 2, SLOTS - 1)),
        ),
        (
            HALVES[0],
            jnp.logical_not(alike),
            ((2, 0, count // 2, PAIRS_AT), (1, count - 1, count % 2, SLOTS - 1)),
        ),
    ):
        for size, offset, trips, slot in steps:

            def step(i, carry):
                at = offset + size * i
                rows = rows_at((start + at) * BLK, size * BLK)
                packed(columns, rows, rows_at(PLEN + CHUNK + at * BLK, size * BLK), slot + i, None)
                return carry

            lax.fori_loop(0, jnp.where(wanted, trips, 0), step, 0)


def main_kernel(me_ref, head_ref, docs, groups, *refs):
    pieces, parts = refs[:9], refs[9:17]
    (weight, forward, q_ref, dq_ref, keep_ref, send_ref,
     held, grads, sems, part_sems, g3, g_ref, delta_ref, lse_ref, tops, totals, weights,
     kall, pkall, vall, pvall, dk, dv, dpk, dpv, dq_acc, o_ref) = refs[17:]
    me = me_ref[0]
    spreads = spread(me, parts, (kall, pkall, vall, pvall), part_sems)
    key_copies = [copy for n, copy in enumerate(spreads) if n % 4 < 2]
    copies = [copy for n, copy in enumerate(spreads) if n % 4 >= 2]
    for k, place in enumerate(PLACES):
        source = pl.multiple_of(head_of(head_ref[0], *place) * DLOC, 128)
        at = pl.ds(k * DLOC, DLOC)
        copies.append(
            pltpu.make_async_copy(weight.at[:, pl.ds(source, DLOC)], held.at[:, at], sems.at[k])
        )
        if k < 7:
            copies.append(pltpu.make_async_copy(pieces[k], grads.at[:, at], sems.at[8 + k]))
    for half in range(2):
        copies.append(
            pltpu.make_async_copy(
                pieces[7 + half],
                grads.at[half * BLK : (half + 1) * BLK, 7 * DLOC :],
                sems.at[15 + half],
            )
        )
    copies.append(pltpu.make_async_copy(forward, o_ref, sems.at[17]))
    for copy in key_copies + copies:
        copy.start()
    for ref in (dk, dv, dpk, dpv, dq_acc):
        ref[...] = jnp.zeros_like(ref)
    for copy in key_copies:
        copy.wait()

    def sums(keys_ref, columns, rows, kept, slot, alike, fresh):
        score = dot(keys_ref[rows, :], q_ref[columns, :], 1, 1) * SCALE2
        if alike is not None:
            score = jnp.where(own_tokens(alike), score, NEGATIVE)
        shape = score.shape
        score = score.reshape(shape[0] // 8, 8, shape[1])
        new = jnp.max(score, axis=0)
        if not fresh:
            top = tops[SLOTS, :, columns]
            new = jnp.maximum(top, new)
        part = jnp.exp2(score - new[None])
        total = jnp.sum(part, axis=0)
        if not fresh:
            total = total + totals[:, columns] * jnp.exp2(top - new)
        weights[kept, columns] = part.reshape(shape).astype(BF)
        totals[:, columns] = total
        tops[slot, :, columns] = new
        tops[SLOTS, :, columns] = new

    def prompt_sums(columns, rows, kept, slot, alike):
        sums(pkall, columns, rows, kept, slot, alike, True)

    def packed_sums(columns, rows, kept, slot, alike):
        sums(kall, columns, rows, kept, slot, alike, False)

    walk(me, docs, groups, prompt_sums, packed_sums)
    top = tops[SLOTS]
    best = jnp.max(top, axis=0, keepdims=True)
    whole = jnp.sum(totals[...] * jnp.exp2(top - best), axis=0, keepdims=True)
    lse_ref[...] = best + jnp.log2(whole)

    for copy in copies:
        copy.wait()
    total = dot(grads[...], held[...], 1, 1)
    for h in range(8):
        g3[:, h, :] = total[:, h * HD : (h + 1) * HD]
    for half, at in enumerate(HALVES):
        low = g3[half * BLK : (half + 1) * BLK].reshape(HALF, HD).astype(BF)
        g_ref[at, :] = low
        product = low.astype(F32) * o_ref[at, :].astype(F32)
        delta_ref[:, at] = jnp.sum(product.T, axis=0, keepdims=True)

    def grads_of(keys_ref, vals_ref, dk_ref, dv_ref, columns, rows, kept, slot):
        g = g_ref[columns, :]
        keys = keys_ref[rows, :]
        dprob = dot(vals_ref[rows, :], g, 1, 1)
        share = jnp.exp2(tops[slot, :, columns] - lse_ref[:, columns])
        share = jnp.concatenate([share, share]).astype(BF)
        part = weights[kept, columns]
        shape = part.shape
        low = (part.reshape(shape[0] // 16, 16, shape[1]) * share[None]).reshape(shape)
        dscore = low * (dprob - delta_ref[:, columns]).astype(BF)
        dv_ref[rows, :] += dot(low, g, 1, 0)
        dk_ref[rows, :] += dot(dscore, q_ref[columns, :], 1, 0)
        dq_acc[:, columns] += dot(keys.T, dscore, 1, 0)

    def prompt_grads(columns, rows, kept, slot, alike):
        grads_of(pkall, pvall, dpk, dpv, columns, rows, kept, slot)

    def packed_grads(columns, rows, kept, slot, alike):
        grads_of(kall, vall, dk, dv, columns, rows, kept, slot)

    walk(me, docs, groups, prompt_grads, packed_grads)
    for at in HALVES:
        dq_ref[at, :] = (dq_acc[:, at].T * FACTOR).astype(BF)

    core = me % 2
    for which, ref in ((core, keep_ref), (1 - core, send_ref)):
        for j in range(8):
            to = 2 * j + which
            big = pl.ds(pl.multiple_of(to * CHUNK, CHUNK), CHUNK)
            small = pl.ds(pl.multiple_of(to * PCHUNK, PCHUNK), PCHUNK)
            ref[j, :CHUNK, :] = dk[big, :].astype(BF)
            ref[j, CHUNK:PIECE, :] = dpk[small, :].astype(BF)
            ref[j, PIECE : PIECE + CHUNK, :] = dv[big, :].astype(BF)
            ref[j, PIECE + CHUNK :, :] = dpv[small, :].astype(BF)


def sum_kernel(terms, k_ref, v_ref, pk_ref, pv_ref):
    total = terms[0].astype(F32)
    for j in range(1, 8):
        total = total + terms[j].astype(F32)
    k_ref[...] = (total[:CHUNK] * FACTOR).astype(BF)
    pk_ref[...] = (total[CHUNK:PIECE] * FACTOR).astype(BF)
    v_ref[...] = total[PIECE : PIECE + CHUNK].astype(BF)
    pv_ref[...] = total[PIECE + CHUNK :].astype(BF)


def vmem():
    return pl.BlockSpec(memory_space=pltpu.VMEM)


def smem():
    return pl.BlockSpec(memory_space=pltpu.SMEM)


def anywhere():
    return pl.BlockSpec(memory_space=pl.ANY)


def per_device(
    queries, keys, values, forward_out, grad_out, out_weight,
    block_docs, doc_group, prefix_keys, prefix_values,
):
    me = lax.axis_index("ctx").astype(jnp.int32).reshape(1)
    head = lax.axis_index("head").astype(jnp.int32).reshape(1)

    own = jnp.concatenate([keys[:, 0], prefix_keys[:, 0], values[:, 0], prefix_values[:, 0]])
    beside = swap_ctx(own, z_swap)
    up = from_head(grad_out, 1, 0)
    down = from_head(grad_out, -1, 0)
    over = from_head(grad_out, 0, 1)
    pair = jnp.stack([own, beside])
    from_next = swap_ctx(pair, x_shift(-1))
    from_prev = swap_ctx(pair, x_shift(1))
    from_far = swap_ctx(pair, x_shift(2))
    over_up = from_head(up, 0, 1)
    over_down = from_head(over, -1, 0)
    far = from_head(up, 1, 0)
    down, over_up, over_down, far = lax.optimization_barrier((down, over_up, over_down, far))
    over_far0 = from_head(over_up[:BLK], 1, 0)
    over_far1 = from_head(over_down[BLK:], -1, 0)
    same = (pair, from_next, from_far, from_prev)
    other = tuple(swap_ctx(piece, core_swap) for piece in same)

    part = jax.ShapeDtypeStruct((8, 2 * PIECE, HD), BF)
    dq, keep, send = pl.pallas_call(
        main_kernel,
        out_shape=(jax.ShapeDtypeStruct((ROWS, HD), BF), part, part),
        in_specs=[smem()] * 4 + [anywhere()] * 19 + [vmem()],
        out_specs=(vmem(),) * 3,
        scratch_shapes=[
            pltpu.VMEM((HALF, 8 * DLOC), BF),
            pltpu.VMEM((CHUNK, 8 * DLOC), BF),
            pltpu.SemaphoreType.DMA((18,)),
            pltpu.SemaphoreType.DMA((64,)),
            pltpu.VMEM((CHUNK, 8, HD), F32),
            pltpu.VMEM((ROWS, HD), BF),
            pltpu.VMEM((1, ROWS), F32),
            pltpu.VMEM((1, ROWS), F32),
            pltpu.VMEM((SLOTS + 1, 8, ROWS), F32),
            pltpu.VMEM((8, ROWS), F32),
            pltpu.VMEM((SPAN, ROWS), BF),
            pltpu.VMEM((TOKENS, HD), BF),
            pltpu.VMEM((PTOK, HD), BF),
            pltpu.VMEM((TOKENS, HD), BF),
            pltpu.VMEM((PTOK, HD), BF),
            pltpu.VMEM((TOKENS, HD), F32),
            pltpu.VMEM((TOKENS, HD), F32),
            pltpu.VMEM((PTOK, HD), F32),
            pltpu.VMEM((PTOK, HD), F32),
            pltpu.VMEM((HD, ROWS), F32),
            pltpu.VMEM((ROWS, HD), BF),
        ],
        compiler_params=pltpu.CompilerParams(vmem_limit_bytes=60 * 1024 * 1024),
        cost_estimate=pl.CostEstimate(flops=10**10, bytes_accessed=10**7, transcendentals=10**7),
        name="attention_grads",
    )(
        me, head, block_docs, doc_group, grad_out, up, down, over, over_up, over_down, far,
        over_far0, over_far1, *same, *other,
        out_weight, forward_out.reshape(ROWS, HD), queries.reshape(ROWS, HD),
    )

    got = swap_ctx(send, core_swap)
    both = (keep.astype(F32) + got.astype(F32)).astype(BF)
    terms = lax.all_to_all(
        both, "ctx", 0, 0, axis_index_groups=[[i for i in range(16) if i % 2 == c] for c in range(2)]
    )
    packed = jax.ShapeDtypeStruct((CHUNK, HD), BF)
    prompt = jax.ShapeDtypeStruct((PCHUNK, HD), BF)
    outs = pl.pallas_call(
        sum_kernel,
        out_shape=(packed, packed, prompt, prompt),
        in_specs=[vmem()],
        out_specs=(vmem(),) * 4,
        name="last_sum",
    )(terms)
    return (dq.reshape(CHUNK, 8, HD), *(out[:, None] for out in outs))


def solution(mesh):
    tokens = P("ctx", "head", None)
    in_specs = (
        tokens, tokens, tokens, tokens, P("ctx", "head"), P("head", None), P(), P(), tokens, tokens,
    )
    return jax.shard_map(
        per_device, mesh=mesh, in_specs=in_specs, out_specs=(tokens,) * 5, check_vma=False
    )
```
